128 devices in a mesh: node: 8 (over x, z_hi), local: 16 (over y, z_lo, core).
Axes of the slice: x: 4, y: 4, z: 4 (z_hi: 2, z_lo: 2; z = z_hi * 2 + z_lo), core: 2. Of those that a mesh axis runs over, the one named last changes fastest.
Arguments:
- context: bfloat16 [8192, 7168], P(('node', 'local')), may hold values from -6 to 6
- cotangent: bfloat16 [8192, 7168], P(('node', 'local')), may hold values from -6 to 6
- weight: bfloat16 [7168, 7168], P(None, 'local'), may hold values from -6 to 6
Outputs:
- input_grad: bfloat16 [8192, 7168], P(('node', 'local'))
- new_weight: float32 [8, 7168, 7168], P('node', None, 'local')
The draws below stay inside these ranges and needn't reach their ends.
All inputs are finite; a program needn't handle non-finite values.
Results may differ from the reference program's by a relative error of at most 0.00165.
Values may be sent and summed in bfloat16 or wider, within the bound.
No kernel may reach another device: no remote copies, remote signals or barrier semaphores. Data moves between devices by JAX's collectives and lax.ppermute only.
A program may use at most 192 MiB of HBM per device.

```python
import jax
import jax.numpy as jnp
from jax import lax

D = 7168
TOKENS = 8192
N_NODE = 8
N_LOCAL = 16


def level_of(rng, extent, pieces, smallest, largest):
    loudness, own = 1.0, jax.random.fold_in(rng, 6)
    for axis_at, shards_of in pieces:
        steps = jnp.exp(jax.random.uniform(jax.random.fold_in(own, axis_at), (shards_of,), jnp.float32, smallest / len(pieces), largest / len(pieces)))
        loudness = loudness * jnp.repeat(steps, extent[axis_at] // shards_of).reshape([-1 if axis == axis_at else 1 for axis in range(len(extent))])
    return loudness


def gaussian(stream_key, extent, deviation, reach, cuts=(), kind=jnp.bfloat16):
    factor_of = level_of(stream_key, extent, cuts, -0.22, 0.18) if cuts else 1.0
    entries = jax.random.normal(stream_key, extent, jnp.float32) * deviation * factor_of
    return jnp.minimum(jnp.maximum(entries, -reach), reach).astype(kind)


def setup_inputs(seed: int = 0) -> dict:
    keys = jax.random.split(jax.random.key(seed), 4)
    return {
        "context": gaussian(keys[0], (TOKENS, D), 1.0, 6.0, ((0, 128),)),
        "cotangent": gaussian(keys[1], (TOKENS, D), 1.0, 6.0, ((0, 128),)),
        "weight": gaussian(keys[2], (D, D), 1.0, 6.0, ((1, 16),)),
    }


def reference(context, cotangent, weight):
    scale = D ** -0.5
    input_grad = (jnp.dot(cotangent, weight.T, preferred_element_type=jnp.float32) * scale).astype(jnp.bfloat16)
    shard = D // N_LOCAL
    tok_node = TOKENS // N_NODE
    ctx = context.astype(jnp.float32).reshape(N_NODE, tok_node, D)
    cot = cotangent.astype(jnp.float32).reshape(N_NODE, tok_node, N_LOCAL, shard)
    wblocks = weight.astype(jnp.float32).reshape(D, N_LOCAL, shard)

    def one_block(index):
        cot_block = lax.dynamic_index_in_dim(cot, index, 2, keepdims=False)
        w_block = lax.dynamic_index_in_dim(wblocks, index, 1, keepdims=False)
        grad = jnp.einsum("ntd,nte->nde", ctx, cot_block, precision=lax.Precision.HIGHEST) * scale
        diff = -0.25 * grad
        low = jnp.min(diff, axis=2, keepdims=True)
        span = jnp.max(diff, axis=2, keepdims=True) - low
        code = (255.0 * (diff - low) / span).astype(jnp.bfloat16)
        decoded = low + code.astype(jnp.float32) * span / 255.0
        mixed = (jnp.roll(decoded, 1, axis=0) + decoded + jnp.roll(decoded, -1, axis=0)) / 3.0
        return w_block[None] + mixed

    blocks = lax.map(one_block, jnp.arange(N_LOCAL, dtype=jnp.int32))
    new_weight = jnp.transpose(blocks, (1, 2, 0, 3)).reshape(N_NODE, D, D)
    return input_grad, new_weight
```

```python
import jax
import jax.numpy as jnp
from jax import lax
from jax.experimental import pallas as pl
from jax.experimental.pallas import tpu as pltpu
from jax.sharding import Mesh, PartitionSpec as P

AXES = ("x", "zh", "y", "zl", "c")
SIZES = (4, 2, 4, 2, 2)
LOCAL = ("y", "zl", "c")

PLAN = (
    (1024, False, "pqz"),
    (1024, False, "pqz"),
    (1024, False, "qpz"),
    (1024, False, "pqz"),
    (1024, True, "zqp"),
    (1024, False, "qpz"),
    (1024, True, "zpq"),
)
SUMS = ((1280, "zqp"), (1152, "pzq"), (1152, "qpz"))


def hop(block, which):
    if which == "p":
        return lax.ppermute(block, "y", [(i, i ^ 1) for i in range(4)])
    if which == "q":
        return lax.ppermute(block, "y", [(i, 3 - i) for i in range(4)])
    if which == "z":
        return lax.ppermute(block, "zl", [(0, 1), (1, 0)])
    if which == "m":
        return lax.ppermute(block, ("zh", "zl"), [(i, 3 - i) for i in range(4)])
    if which == "h":
        return lax.ppermute(block, "zh", [(0, 1), (1, 0)])
    if which == "x":
        route = [(2 * i, 2 * ((i + 1) % 4)) for i in range(4)]
        route += [(2 * i + 1, 2 * ((i + 3) % 4) + 1) for i in range(4)]
        return lax.ppermute(block, ("x", "zh"), route)
    return lax.ppermute(block, "c", [(0, 1), (1, 0)])


AXIS_OF = {"z": 0, "q": 1, "p": 2}


def gather_rows(block, order):
    r, t, w = block.shape
    held = block.reshape(r, 1, 1, 1, t, w)
    for which in order:
        held = jnp.concatenate([held, hop(held, which)], axis=1 + AXIS_OF[which])
    return held.reshape(r, 8 * t, w)


def context_chunk(block, early, order):
    block = block[None]
    if early:
        second = hop(block, "m")
        third = hop(second, "x")
        own = gather_rows(jnp.concatenate([block, second, third], axis=0), order)
        other = hop(own, "c")
        return [(own[i], other[i]) for i in range(3)]
    first = gather_rows(block, order)[0]
    second = hop(first, "m")
    third = hop(second, "x")
    return [(part, hop(part, "c")) for part in (first, second, third)]


def update_kernel(scale, n_parts, stacked, *refs):
    cots = refs[:3]
    if stacked:
        own_ref, other_ref = refs[3:5]
        parts = [(own_ref[i], other_ref[i]) for i in range(3)]
        weight_ref = refs[5]
    else:
        parts = [(refs[3 + 2 * i][...], refs[4 + 2 * i][...]) for i in range(3)]
        weight_ref = refs[9]
    out_ref = refs[-1]
    total = weight_ref[...].astype(jnp.float32)
    for cot_ref, (own, other) in zip(cots, parts):
        half = own.shape[0]
        g = jnp.dot(cot_ref[:, :half], own, preferred_element_type=jnp.float32)
        g += jnp.dot(cot_ref[:, half:], other, preferred_element_type=jnp.float32)
        top = jnp.max(g, axis=0, keepdims=True)
        spread = top - jnp.min(g, axis=0, keepdims=True)
        code = (((top - g) * (1.0 / spread)) * 255.0).astype(jnp.bfloat16)
        low = top * (-0.25 * scale / 3.0)
        step = spread * (0.25 * scale / (3.0 * 255.0))
        total += low + code.astype(jnp.float32) * step
    out_ref[...] = total


def update(cots, parts, stacked, weight_t, out, first_column, width, tile, scale):
    rows, columns = weight_t.shape
    tokens = cots[0].shape[1]
    base = first_column // tile
    whole = pl.BlockSpec((rows, tokens), lambda j: (0, 0))
    if stacked:
        part_spec = [pl.BlockSpec((3, tokens // 2, tile), lambda j: (0, 0, j))] * 2
    else:
        part_spec = [pl.BlockSpec((tokens // 2, tile), lambda j: (0, j))] * 6
    here = pl.BlockSpec((rows, tile), lambda j: (0, base + j))
    args = [*cots, *parts, weight_t]
    specs = [whole] * 3 + part_spec + [here]
    aliases = {}
    if out is not None:
        aliases = {len(args): 0}
        args.append(out)
        specs.append(pl.BlockSpec(memory_space=pl.ANY))
    return pl.pallas_call(
        lambda *refs: update_kernel(scale, 3, stacked, *refs),
        grid=(width // tile,),
        in_specs=specs,
        out_specs=here,
        out_shape=jax.ShapeDtypeStruct((rows, columns), jnp.float32),
        input_output_aliases=aliases,
        compiler_params=pltpu.CompilerParams(
            dimension_semantics=("arbitrary",), vmem_limit_bytes=40 * 2**20
        ),
        cost_estimate=pl.CostEstimate(
            flops=3 * 2 * rows * tokens * width * 2,
            bytes_accessed=3 * tokens * width * 2 + rows * width * 6,
            transcendentals=0,
        ),
    )(*args)


def body(context, cotangent, weight):
    tokens, width = context.shape
    scale = width ** (-0.5)
    y, zl, c = (lax.axis_index(name) for name in LOCAL)
    weight_t = weight.T
    block = weight_t.shape[0]
    half = width // 2

    sizes = jnp.stack([
        jnp.max(jnp.abs(cotangent)).astype(jnp.float32),
        jnp.max(jnp.abs(weight_t)).astype(jnp.float32),
    ])
    sizes = jnp.maximum(lax.pmax(sizes, LOCAL), 2.0**-120)
    cot_size, weight_size = sizes[0], sizes[1]

    weight_own = lax.dynamic_slice_in_dim(weight_t, c * half, half, axis=1)
    weight_other = hop(lax.dynamic_slice_in_dim(weight_t, (1 - c) * half, half, axis=1), "c")

    blocks = lax.all_to_all(
        cotangent.reshape(tokens, 16, block).transpose(1, 0, 2), LOCAL, split_axis=0, concat_axis=0, tiled=True
    )
    picked = [
        lax.dynamic_index_in_dim(blocks, (y ^ (p ^ (3 * q))) * 4 + (zl ^ jz) * 2 + (c ^ jc), 0, keepdims=False)
        for jc in range(2) for jz in range(2) for q in range(2) for p in range(2)
    ]
    cot = jnp.concatenate(picked, axis=0)
    rows = cot.shape[0]
    cot_other = hop(cot, "c")
    cot_other = jnp.concatenate([cot_other[rows // 2:], cot_other[: rows // 2]], axis=0)
    cot_t = cot.T
    quarter = rows // 4
    second_t = hop(cot_t, "h")
    second_t = jnp.concatenate(
        [second_t[:, i * quarter:(i + 1) * quarter] for i in (1, 0, 3, 2)], axis=1
    )
    third_t = hop(second_t, "x")
    cots = (cot_t, second_t, third_t)

    finished = []
    start = 0
    for columns, order in SUMS:
        cols = slice(start, start + columns)
        start += columns
        part = jnp.dot(cot, weight_own[:, cols], preferred_element_type=jnp.float32)
        part += jnp.dot(cot_other, weight_other[:, cols], preferred_element_type=jnp.float32)
        held = ((part * (1.0 / cot_size)) * (1.0 / weight_size)).astype(jnp.float16)
        held = held.reshape(2, 2, 2, 2, tokens, columns)
        for which in order:
            axis = 1 + AXIS_OF[which]
            keep, send = lax.index_in_dim(held, 0, axis), lax.index_in_dim(held, 1, axis)
            held = keep.astype(jnp.float32) + hop(send.astype(jnp.float16), which).astype(jnp.float32)
        finished.append(held.reshape(2, tokens, columns))
    summed = jnp.concatenate(finished, axis=2) * (cot_size * scale) * weight_size
    summed = summed.astype(jnp.bfloat16)
    arrived = hop(summed[1], "c")
    input_grad = jnp.where(
        c == 0,
        jnp.concatenate([summed[0], arrived], axis=1),
        jnp.concatenate([arrived, summed[0]], axis=1),
    )

    out = None
    start = 0
    for columns, early, order in PLAN:
        parts = context_chunk(context[:, start:start + columns], early, order)
        if early:
            pass
        flat = [half_part for pair in parts for half_part in pair]
        out = update(cots, flat, False, weight_t, out, start, columns, 512, scale)
        start += columns
    return input_grad, out.T[None]


def solution(mesh):
    sub = Mesh(mesh.devices.reshape(SIZES), AXES)
    tokens = P(AXES, None)
    return jax.shard_map(
        body,
        mesh=sub,
        in_specs=(tokens, tokens, P(None, LOCAL)),
        out_specs=(tokens, P(("x", "zh"), None, LOCAL)),
        check_vma=False,
    )
```

```python
import jax
import jax.numpy as jnp
from jax import lax
from jax.experimental import pallas as pl
from jax.experimental.pallas import tpu as pltpu
from jax.sharding import Mesh, PartitionSpec as P

AXES = ("x", "zh", "y", "zl", "c")
SIZES = (4, 2, 4, 2, 2)
LOCAL = ("y", "zl", "c")

CHUNKS = (1024,) * 7
GATHERS = (((0, 1), 0, 0), ((2, 3, 4), 1, 2), ((5, 6), 3, 4))
SUMS = ((1792, 2, 4, 5), (1792, 3, 6, 7))


def hop(block, which):
    if which == "p":
        return lax.ppermute(block, "y", [(i, i ^ 1) for i in range(4)])
    if which == "q":
        return lax.ppermute(block, "y", [(i, 3 - i) for i in range(4)])
    if which == "z":
        return lax.ppermute(block, "zl", [(0, 1), (1, 0)])
    if which == "m":
        return lax.ppermute(block, ("zh", "zl"), [(i, 3 - i) for i in range(4)])
    if which == "h":
        return lax.ppermute(block, "zh", [(0, 1), (1, 0)])
    if which == "x":
        route = [(2 * i, 2 * ((i + 1) % 4)) for i in range(4)]
        route += [(2 * i + 1, 2 * ((i + 3) % 4) + 1) for i in range(4)]
        return lax.ppermute(block, ("x", "zh"), route)
    return lax.ppermute(block, "c", [(0, 1), (1, 0)])


def update_kernel(scale, core, cot1, cot2, cot3, first, own2, own3, other2, other3, weight_ref, *rest):
    out_ref, *products = rest[-4:]
    rows = out_ref.shape[0]
    step_rows = 32

    def run(second, third):
        stats = []
        for g, cot_ref, rows_ref in zip(products, (cot1, cot2, cot3), (first, second, third)):
            g[...] = jnp.dot(cot_ref[...], rows_ref[...], preferred_element_type=jnp.float32)
        for g in products:
            top = bottom = g[0:8, :]
            for r in range(8, rows, 8):
                piece = g[r:r + 8, :]
                top, bottom = jnp.maximum(top, piece), jnp.minimum(bottom, piece)
            top = jnp.max(top, axis=0, keepdims=True)
            spread = top - jnp.min(bottom, axis=0, keepdims=True)
            stats.append((top, 1.0 / spread, spread * (0.25 * scale / (3.0 * 255.0))))
        low = sum(top for top, _, _ in stats) * (-0.25 * scale / 3.0)
        for r in range(0, rows, step_rows):
            here = slice(r, r + step_rows)
            total = weight_ref[here, :].astype(jnp.float32) + low
            for g, (top, inverse, step) in zip(products, stats):
                code = (((top - g[here, :]) * inverse) * 255.0).astype(jnp.bfloat16)
                total += code.astype(jnp.float32) * step
            out_ref[here, :] = total

    @pl.when(pl.program_id(0) == 0)
    def _():
        run(own2, own3)

    @pl.when(pl.program_id(0) == 1)
    def _():
        run(other2, other3)


def update(core, cots, first, offset, own2, own3, other2, other3, weight_t, out, first_column, tile, scale):
    rows, columns = weight_t.shape
    tokens, width = own2.shape[0], 2 * own2.shape[1]
    tiles = width // 2 // tile
    base = first_column // tile

    def half_at(i, j, core):
        return (core[0] ^ i) * tiles + j

    whole = pl.BlockSpec((rows, tokens), lambda i, j, core: (0, 0))
    mine = pl.BlockSpec((tokens, tile), lambda i, j, core: (0, jnp.where(i == 0, j, tiles - 1)))
    theirs = pl.BlockSpec((tokens, tile), lambda i, j, core: (0, jnp.where(i == 0, 0, j)))
    here = pl.BlockSpec((rows, tile), lambda i, j, core: (0, base + half_at(i, j, core)))
    args = [core, *cots, first, own2, own3, other2, other3, weight_t]
    specs = [whole] * 3 + [pl.BlockSpec((tokens, tile), lambda i, j, core: (0, offset // tile + half_at(i, j, core)))]
    specs += [mine] * 2 + [theirs] * 2 + [here]
    aliases = {}
    if out is not None:
        aliases = {len(args): 0}
        args.append(out)
        specs.append(pl.BlockSpec(memory_space=pl.ANY))
    return pl.pallas_call(
        lambda *refs: update_kernel(scale, *refs),
        grid_spec=pltpu.PrefetchScalarGridSpec(
            num_scalar_prefetch=1, grid=(2, tiles), in_specs=specs, out_specs=here,
            scratch_shapes=[pltpu.VMEM((rows, tile), jnp.float32)] * 3,
        ),
        out_shape=jax.ShapeDtypeStruct((rows, columns), jnp.float32),
        input_output_aliases=aliases,
        compiler_params=pltpu.CompilerParams(
            dimension_semantics=("arbitrary", "arbitrary"), vmem_limit_bytes=60 * 2**20
        ),
        cost_estimate=pl.CostEstimate(
            flops=3 * 2 * rows * tokens * width,
            bytes_accessed=3 * tokens * width * 2 + rows * width * 6,
            transcendentals=0,
        ),
    )(*args)


def body(context, cotangent, weight):
    tokens, width = context.shape
    scale = width ** (-0.5)
    c = lax.axis_index("c")
    weight_t = weight.T
    block = weight_t.shape[0]
    half = width // 2
    core = c.astype(jnp.int32)[None]

    n = len(CHUNKS)
    starts = [sum(CHUNKS[:i]) for i in range(n)]
    sum_starts = [sum(s[0] for s in SUMS[:i]) for i in range(len(SUMS))]
    group_of = {k: g for g, (ks, _, _) in enumerate(GATHERS) for k in ks}
    offset = {k: starts[k] - starts[GATHERS[group_of[k]][0][0]] for k in range(n)}

    def piece(g, context):
        first, last = GATHERS[g][0][0], GATHERS[g][0][-1]
        return context[:, starts[first]:starts[last] + CHUNKS[last]]

    def half_of(k, gathered):
        first, middle, end = offset[k], offset[k] + CHUNKS[k] // 2, offset[k] + CHUNKS[k]
        return jnp.where(c == 0, gathered[:, first:middle], gathered[:, middle:end])

    live, flying = {"context": context, "weight": weight_t}, {}
    for slot in range(n + 3):
        new = {}
        for g, (_, begin, end) in enumerate(GATHERS):
            if slot == max(begin - 1, 0):
                new["piece", g] = piece(g, live["context"])
            if slot == begin:
                ready = live["piece", g] if ("piece", g) in live else new["piece", g]
                flying["first", g] = lax.all_gather(ready, LOCAL, axis=0, tiled=True)
            if slot == end:
                new["first", g] = flying.pop(("first", g))
        k = slot - 1
        if 0 <= k < n:
            new["own2", k] = hop(live["half", k], "m")
        k = slot - 2
        if 0 <= k < n:
            new["own3", k] = hop(live["own2", k], "x")
            new["other2", k] = hop(live["own2", k], "c")
        k = slot - 3
        if 0 <= k < n:
            new["other3", k] = hop(live["own3", k], "c")
        k = slot
        if k < n:
            at = group_of[k]
            new["half", k] = half_of(k, live["first", at] if ("first", at) in live else new["first", at])
        for k in range(n):
            if slot == (k + 4 if k < n - 3 else k + 3):
                first, own2, own3, other2 = (live[name, k] for name in ("own2", "own2", "own3", "other2"))
                first = live["first", group_of[k]]
                other3 = live["other3", k] if ("other3", k) in live else new["other3", k]
                new["out"] = update(
                    core, live["cots"], first, offset[k], own2, own3, other2, other3, live["weight"],
                    new.get("out", live.get("out")), starts[k], 512, scale
                )

        if slot == 0:
            def columns_of(shard):
                by_block = shard.reshape(tokens, 16, block).transpose(1, 0, 2)
                blocks = lax.all_to_all(by_block, LOCAL, split_axis=0, concat_axis=0, tiled=True)
                return blocks

            cot2 = hop(cotangent, "m")
            new["cot"] = columns_of(cotangent).reshape(16 * tokens, block)
            new["cot_t"] = new["cot"].T
            blocks = columns_of(cot2).reshape(4, 2, 2 * tokens, block)
            new["cot2_t"] = jnp.stack([blocks[:, 1], blocks[:, 0]], axis=1).reshape(16 * tokens, block).T
            new["weight_sent"] = jnp.where(c == 0, weight_t[:, half:], weight_t[:, :half])
            sizes = jnp.stack([jnp.max(jnp.abs(cotangent)), jnp.max(jnp.abs(weight_t))]).astype(jnp.float32)
            new["sizes"] = jnp.broadcast_to(jnp.maximum(sizes, 2.0**-120)[:, None], (2, 128))
        if slot == 1:
            new["cots"] = (live["cot_t"], live["cot2_t"], hop(live["cot2_t"], "x"))
            new["both_cots"] = jnp.concatenate([live["cot"], hop(live["cot"], "c")], axis=1)
            weight_own = jnp.where(c == 0, live["weight"][:, :half], live["weight"][:, half:])
            new["both_weights"] = jnp.concatenate([weight_own, hop(live["weight_sent"], "c")], axis=0)
            sizes = live["sizes"]
            for which in "czpq":
                sizes = jnp.maximum(sizes, hop(sizes, which))
            new["sizes"] = sizes
        if slot > 1:
            cot_size, weight_size = live["sizes"][0, 0], live["sizes"][1, 0]
        for i, (columns, made, begin, end) in enumerate(SUMS):
            if slot == made:
                part = jnp.dot(
                    live["both_cots"], live["both_weights"][:, sum_starts[i]:sum_starts[i] + columns],
                    preferred_element_type=jnp.float32
                )
                part = (part * (1.0 / cot_size)) * (1.0 / weight_size)
                new["part", i] = part.astype(jnp.float16).reshape(8, 2 * tokens, columns)
            if slot == begin:
                flying["sent", i] = lax.all_to_all(live["part", i], ("y", "zl"), split_axis=0, concat_axis=0, tiled=True)
            if slot == end:
                new["sent", i] = flying.pop(("sent", i))
            if slot == end + 1:
                total = jnp.sum(live["sent", i].astype(jnp.float32), axis=0) * (cot_size * scale) * weight_size
                new["sum", i] = total.astype(jnp.bfloat16)
        if slot == n + 2:
            summed = jnp.concatenate([live["sum", i] for i in range(len(SUMS))], axis=1)
            mine = lax.dynamic_slice_in_dim(summed, c * tokens, tokens, axis=0)
            arrived = hop(lax.dynamic_slice_in_dim(summed, (1 - c) * tokens, tokens, axis=0), "c")
            new["input_grad"] = jnp.where(
                c == 0,
                jnp.concatenate([mine, arrived], axis=1),
                jnp.concatenate([arrived, mine], axis=1),
            )
        live.update(new)
        if slot < n + 2:
            names = list(live)
            live = dict(zip(names, lax.optimization_barrier(tuple(live[name] for name in names))))
    return live["input_grad"], live["out"].T[None]


def solution(mesh):
    sub = Mesh(mesh.devices.reshape(SIZES), AXES)
    tokens = P(AXES, None)
    return jax.shard_map(
        body,
        mesh=sub,
        in_specs=(tokens, tokens, P(None, LOCAL)),
        out_specs=(tokens, P(("x", "zh"), None, LOCAL)),
        check_vma=False,
    )
```

```python
import jax
import jax.numpy as jnp
from jax import lax
from jax.experimental import pallas as pl
from jax.experimental.pallas import tpu as pltpu
from jax.sharding import Mesh, PartitionSpec as P

AXES = ("x", "zh", "y", "zl", "c")
SIZES = (4, 2, 4, 2, 2)
LOCAL = ("y", "zl", "c")

CHUNKS = (1024,) * 6
GATHERS = (((0, 1), 0, 0), ((2, 3, 4), 1, 2), ((5,), 3, 5))
TOGETHER = (4, 6)
SUMS = ((1536, 3, 3, 5), (2048, 4, 6, 7))


def hop(block, which):
    if which == "p":
        return lax.ppermute(block, "y", [(i, i ^ 1) for i in range(4)])
    if which == "q":
        return lax.ppermute(block, "y", [(i, 3 - i) for i in range(4)])
    if which == "z":
        return lax.ppermute(block, "zl", [(0, 1), (1, 0)])
    if which == "m":
        return lax.ppermute(block, ("zh", "zl"), [(i, 3 - i) for i in range(4)])
    if which == "h":
        return lax.ppermute(block, "zh", [(0, 1), (1, 0)])
    if which == "x":
        route = [(2 * i, 2 * ((i + 1) % 4)) for i in range(4)]
        route += [(2 * i + 1, 2 * ((i + 3) % 4) + 1) for i in range(4)]
        return lax.ppermute(block, ("x", "zh"), route)
    return lax.ppermute(block, "c", [(0, 1), (1, 0)])


def new_columns(scale, weight_ref, out_ref, products):
    rows = out_ref.shape[0]
    step_rows = 32
    stats = []
    for g in products:
        top = bottom = g[0:8, :]
        for r in range(8, rows, 8):
            piece = g[r:r + 8, :]
            top, bottom = jnp.maximum(top, piece), jnp.minimum(bottom, piece)
        top = jnp.max(top, axis=0, keepdims=True)
        spread = top - jnp.min(bottom, axis=0, keepdims=True)
        stats.append((top, 1.0 / spread, spread * (0.25 * scale / (3.0 * 255.0))))
    low = sum(top for top, _, _ in stats) * (-0.25 * scale / 3.0)
    for r in range(0, rows, step_rows):
        here = slice(r, r + step_rows)
        total = weight_ref[here, :].astype(jnp.float32) + low
        for g, (top, inverse, step) in zip(products, stats):
            code = (((top - g[here, :]) * inverse) * 255.0).astype(jnp.bfloat16)
            total += code.astype(jnp.float32) * step
        out_ref[here, :] = total


def update_kernel(scale, core, cot1, cot2, cot3, first, own2, own3, other2, other3, weight_ref, *rest):
    out_ref, *products = rest[-4:]

    def run(second, third):
        for g, cot_ref, rows_ref in zip(products, (cot1, cot2, cot3), (first, second, third)):
            g[...] = jnp.dot(cot_ref[...], rows_ref[...], preferred_element_type=jnp.float32)
        new_columns(scale, weight_ref, out_ref, products)

    @pl.when(pl.program_id(0) == 0)
    def _():
        run(own2, own3)

    @pl.when(pl.program_id(0) == 1)
    def _():
        run(other2, other3)


def together_kernel(scale, cot1, cot2, cot3, first, second, third, weight_ref, *rest):
    out_ref, *products = rest[-4:]
    tokens = cot1.shape[1]
    n = tokens // 8
    for g, cot_ref, rows_ref, swap in zip(products, (cot1, cot2, cot3), (first, second, third), (0, 1, 1)):
        cot = cot_ref[...]
        if swap:
            cot = jnp.concatenate([cot[:, (i ^ 1) * n:((i ^ 1) + 1) * n] for i in range(8)], axis=1)
        rows = rows_ref[...].reshape(tokens, rows_ref.shape[-1])
        g[...] = jnp.dot(cot, rows, preferred_element_type=jnp.float32)
    new_columns(scale, weight_ref, out_ref, products)


def update_together(cots, gathered, weight_t, out, first_column, tile, scale):
    rows, columns = weight_t.shape
    n, _, t, width = gathered.shape
    base = first_column // tile
    whole = pl.BlockSpec((rows, n * t), lambda j: (0, 0))
    here = pl.BlockSpec((rows, tile), lambda j: (0, base + j))
    parts = [pl.BlockSpec((n, 1, t, tile), lambda j, r=r: (0, r, 0, j)) for r in range(3)]
    return pl.pallas_call(
        lambda *refs: together_kernel(scale, *refs),
        grid=(width // tile,),
        in_specs=[whole] * 3 + parts + [here, pl.BlockSpec(memory_space=pl.ANY)],
        out_specs=here,
        out_shape=jax.ShapeDtypeStruct((rows, columns), jnp.float32),
        scratch_shapes=[pltpu.VMEM((rows, tile), jnp.float32)] * 3,
        input_output_aliases={7: 0},
        compiler_params=pltpu.CompilerParams(dimension_semantics=("arbitrary",), vmem_limit_bytes=60 * 2**20),
        cost_estimate=pl.CostEstimate(
            flops=3 * 2 * rows * n * t * width, bytes_accessed=3 * n * t * width * 2 + rows * width * 6, transcendentals=0
        ),
    )(*cots, gathered, gathered, gathered, weight_t, out)


def update(core, cots, first, offset, own2, own3, other2, other3, weight_t, out, first_column, tile, scale):
    rows, columns = weight_t.shape
    tokens, width = own2.shape[0], 2 * own2.shape[1]
    tiles = width // 2 // tile
    base = first_column // tile

    def half_at(i, j, core):
        return (core[0] ^ i) * tiles + j

    whole = pl.BlockSpec((rows, tokens), lambda i, j, core: (0, 0))
    mine = pl.BlockSpec((tokens, tile), lambda i, j, core: (0, jnp.where(i == 0, j, tiles - 1)))
    theirs = pl.BlockSpec((tokens, tile), lambda i, j, core: (0, jnp.where(i == 0, 0, j)))
    here = pl.BlockSpec((rows, tile), lambda i, j, core: (0, base + half_at(i, j, core)))
    args = [core, *cots, first, own2, own3, other2, other3, weight_t]
    specs = [whole] * 3 + [pl.BlockSpec((tokens, tile), lambda i, j, core: (0, offset // tile + half_at(i, j, core)))]
    specs += [mine] * 2 + [theirs] * 2 + [here]
    aliases = {}
    if out is not None:
        aliases = {len(args): 0}
        args.append(out)
        specs.append(pl.BlockSpec(memory_space=pl.ANY))
    return pl.pallas_call(
        lambda *refs: update_kernel(scale, *refs),
        grid_spec=pltpu.PrefetchScalarGridSpec(
            num_scalar_prefetch=1, grid=(2, tiles), in_specs=specs, out_specs=here,
            scratch_shapes=[pltpu.VMEM((rows, tile), jnp.float32)] * 3,
        ),
        out_shape=jax.ShapeDtypeStruct((rows, columns), jnp.float32),
        input_output_aliases=aliases,
        compiler_params=pltpu.CompilerParams(
            dimension_semantics=("arbitrary", "arbitrary"), vmem_limit_bytes=60 * 2**20
        ),
        cost_estimate=pl.CostEstimate(
            flops=3 * 2 * rows * tokens * width,
            bytes_accessed=3 * tokens * width * 2 + rows * width * 6,
            transcendentals=0,
        ),
    )(*args)


def body(context, cotangent, weight):
    tokens, width = context.shape
    scale = width ** (-0.5)
    c = lax.axis_index("c")
    weight_t = weight.T
    block = weight_t.shape[0]
    half = width // 2
    core = c.astype(jnp.int32)[None]

    n = len(CHUNKS)
    starts = [sum(CHUNKS[:i]) for i in range(n)]
    sum_starts = [sum(s[0] for s in SUMS[:i]) for i in range(len(SUMS))]
    group_of = {k: g for g, (ks, _, _) in enumerate(GATHERS) for k in ks}
    offset = {k: starts[k] - starts[GATHERS[group_of[k]][0][0]] for k in range(n)}

    def piece(g, context):
        first, last = GATHERS[g][0][0], GATHERS[g][0][-1]
        return context[:, starts[first]:starts[last] + CHUNKS[last]]

    def half_of(k, gathered):
        first, middle, end = offset[k], offset[k] + CHUNKS[k] // 2, offset[k] + CHUNKS[k]
        return jnp.where(c == 0, gathered[:, first:middle], gathered[:, middle:end])

    live, flying = {"context": context, "cotangent": cotangent, "weight": weight_t}, {}
    for slot in range(n + 3):
        new = {}
        def get(*name):
            name = name if len(name) > 1 else name[0]
            return new[name] if name in new else live[name]

        for g, (_, begin, end) in enumerate(GATHERS):
            if slot == max(begin - 1, 0):
                new["piece", g] = piece(g, live["context"])
            if slot == begin:
                ready = live["piece", g] if ("piece", g) in live else new["piece", g]
                flying["first", g] = lax.all_gather(ready, LOCAL, axis=0, tiled=True)
            if slot == end:
                new["first", g] = flying.pop(("first", g))
        k = slot - 1
        if 0 <= k < n:
            new["own2", k] = hop(live["half", k], "m")
        k = slot - 2
        if 0 <= k < n:
            new["own3", k] = hop(live["own2", k], "x")
            new["other2", k] = hop(live["own2", k], "c")
        k = slot - 3
        if 0 <= k < n:
            new["other3", k] = hop(live["own3", k], "c")
        k = slot
        if k < n:
            at = group_of[k]
            new["half", k] = half_of(k, live["first", at] if ("first", at) in live else new["first", at])
        for k in range(n):
            if slot == (k + 4 if k < n - 3 else k + 3):
                first, own2, own3, other2 = (live[name, k] for name in ("own2", "own2", "own3", "other2"))
                first = live["first", group_of[k]]
                other3 = live["other3", k] if ("other3", k) in live else new["other3", k]
                new["out"] = update(
                    core, live["cots"], first, offset[k], own2, own3, other2, other3, live["weight"],
                    new.get("out", live.get("out")), starts[k], 512, scale
                )

        if slot == 0:
            new["rows2"] = hop(context[:, sum(CHUNKS):], "m")
        if slot == 1:
            new["rows3"] = hop(live["rows2"], "x")
        if slot == 2:
            new["rows"] = jnp.stack([live["context"][:, sum(CHUNKS):], live["rows2"], live["rows3"]])
        if slot == TOGETHER[0]:
            flying["together"] = lax.all_gather(live["rows"], LOCAL, axis=0, tiled=False)
        if slot == TOGETHER[1]:
            new["together"] = flying.pop("together")
        if slot == TOGETHER[1] + 1:
            new["out"] = update_together(
                live["cots"], live["together"], live["weight"], get("out"), sum(CHUNKS), 512, scale
            )

        if slot == 0:
            def columns_of(shard):
                by_block = shard.reshape(tokens, 16, block).transpose(1, 0, 2)
                blocks = lax.all_to_all(by_block, LOCAL, split_axis=0, concat_axis=0, tiled=True)
                return blocks

            cot2 = hop(cotangent, "m")
            blocks = columns_of(cot2).reshape(4, 2, 2 * tokens, block)
            new["cot2_t"] = jnp.stack([blocks[:, 1], blocks[:, 0]], axis=1).reshape(16 * tokens, block).T
            new["weight_sent"] = jnp.where(c == 0, weight_t[:, half:], weight_t[:, :half])
            sizes = jnp.stack([jnp.max(jnp.abs(cotangent)), jnp.max(jnp.abs(weight_t))]).astype(jnp.float32)
            sizes = jnp.broadcast_to(jnp.maximum(sizes, 2.0**-120)[:, None], (2, 128))
            for which in "czpq":
                sizes = jnp.maximum(sizes, hop(sizes, which))
            new["sizes"] = sizes
        if slot == 1:
            new["cot3_t"] = hop(live["cot2_t"], "x")
            weight_own = jnp.where(c == 0, live["weight"][:, :half], live["weight"][:, half:])
            new["both_weights"] = jnp.concatenate([weight_own, hop(live["weight_sent"], "c")], axis=0)
        if slot == 2:
            new["cot"] = columns_of(live["cotangent"]).reshape(16 * tokens, block)
        if slot == 3:
            new["cots"] = (live["cot"].T, live["cot2_t"], live["cot3_t"])
            new["both_cots"] = jnp.concatenate([live["cot"], hop(live["cot"], "c")], axis=1)
        if slot > 1:
            cot_size, weight_size = live["sizes"][0, 0], live["sizes"][1, 0]
        for i, (columns, made, begin, end) in enumerate(SUMS):
            if slot == made:
                part = jnp.dot(
                    get("both_cots"), live["both_weights"][:, sum_starts[i]:sum_starts[i] + columns],
                    preferred_element_type=jnp.float32
                )
                part = (part * (1.0 / cot_size)) * (1.0 / weight_size)
                new["part", i] = part.astype(jnp.float16).reshape(8, 2 * tokens, columns)
            if slot == begin:
                flying["sent", i] = lax.all_to_all(get("part", i), ("y", "zl"), split_axis=0, concat_axis=0, tiled=True)
            if slot == end:
                new["sent", i] = flying.pop(("sent", i))
            if slot == end + 1:
                total = jnp.sum(live["sent", i].astype(jnp.float32), axis=0) * (cot_size * scale) * weight_size
                new["sum", i] = total.astype(jnp.bfloat16)
        if slot == n + 2:
            summed = jnp.concatenate([get("sum", i) for i in range(len(SUMS))], axis=1)
            mine = lax.dynamic_slice_in_dim(summed, c * tokens, tokens, axis=0)
            arrived = hop(lax.dynamic_slice_in_dim(summed, (1 - c) * tokens, tokens, axis=0), "c")
            new["input_grad"] = jnp.where(
                c == 0,
                jnp.concatenate([mine, arrived], axis=1),
                jnp.concatenate([arrived, mine], axis=1),
            )
        live.update(new)
        if slot < n + 2:
            names = list(live)
            live = dict(zip(names, lax.optimization_barrier(tuple(live[name] for name in names))))
    return live["input_grad"], live["out"].T[None]


def solution(mesh):
    sub = Mesh(mesh.devices.reshape(SIZES), AXES)
    tokens = P(AXES, None)
    return jax.shard_map(
        body,
        mesh=sub,
        in_specs=(tokens, tokens, P(None, LOCAL)),
        out_specs=(tokens, P(("x", "zh"), None, LOCAL)),
        check_vma=False,
    )
```

```python
import jax
import jax.numpy as jnp
from jax import lax
from jax.experimental import pallas as pl
from jax.experimental.pallas import tpu as pltpu
from jax.sharding import Mesh, PartitionSpec as P

AXES = ("x", "zh", "y", "zl", "c")
SIZES = (4, 2, 4, 2, 2)
LOCAL = ("y", "zl", "c")

CHUNKS = (1024,) * 6
GATHERS = (((0, 1), 0, 0), ((2, 3, 4), 1, 2), ((5,), 3, 5))
TOGETHER = (4, 6)
SUMS = ((1536, 3, 3, 5), (2048, 4, 6, 7))


def hop(block, which):
    if which == "p":
        return lax.ppermute(block, "y", [(i, i ^ 1) for i in range(4)])
    if which == "q":
        return lax.ppermute(block, "y", [(i, 3 - i) for i in range(4)])
    if which == "z":
        return lax.ppermute(block, "zl", [(0, 1), (1, 0)])
    if which == "m":
        return lax.ppermute(block, ("zh", "zl"), [(i, 3 - i) for i in range(4)])
    if which == "h":
        return lax.ppermute(block, "zh", [(0, 1), (1, 0)])
    if which == "x":
        route = [(2 * i, 2 * ((i + 1) % 4)) for i in range(4)]
        route += [(2 * i + 1, 2 * ((i + 3) % 4) + 1) for i in range(4)]
        return lax.ppermute(block, ("x", "zh"), route)
    return lax.ppermute(block, "c", [(0, 1), (1, 0)])


def new_columns(scale, weight_ref, out_ref, products):
    rows = out_ref.shape[0]
    step_rows = 32
    stats = []
    for g in products:
        top = bottom = g[0:8, :]
        for r in range(8, rows, 8):
            piece = g[r:r + 8, :]
            top, bottom = jnp.maximum(top, piece), jnp.minimum(bottom, piece)
        top = jnp.max(top, axis=0, keepdims=True)
        spread = top - jnp.min(bottom, axis=0, keepdims=True)
        stats.append((top, 1.0 / spread, spread * (0.25 * scale / (3.0 * 255.0))))
    low = sum(top for top, _, _ in stats) * (-0.25 * scale / 3.0)
    for r in range(0, rows, step_rows):
        here = slice(r, r + step_rows)
        total = weight_ref[here, :].astype(jnp.float32) + low
        for g, (top, inverse, step) in zip(products, stats):
            code = (((top - g[here, :]) * inverse) * 255.0).astype(jnp.bfloat16)
            total += code.astype(jnp.float32) * step
        out_ref[here, :] = total


def update_kernel(scale, core, cot1, cot2, cot3, first, own2, own3, other2, other3, weight_ref, *rest):
    out_ref, *products = rest[-4:]

    def run(second, third):
        for g, cot_ref, rows_ref in zip(products, (cot1, cot2, cot3), (first, second, third)):
            g[...] = jnp.dot(cot_ref[...], rows_ref[...], preferred_element_type=jnp.float32)
        new_columns(scale, weight_ref, out_ref, products)

    @pl.when(pl.program_id(0) == 0)
    def _():
        run(own2, own3)

    @pl.when(pl.program_id(0) == 1)
    def _():
        run(other2, other3)


def together_kernel(scale, cot1, cot2, cot3, first, second, third, weight_ref, *rest):
    out_ref, *products = rest[-4:]
    tokens = cot1.shape[1]
    n = tokens // 8
    for g, cot_ref, rows_ref, swap in zip(products, (cot1, cot2, cot3), (first, second, third), (0, 1, 1)):
        cot = cot_ref[...]
        if swap:
            cot = jnp.concatenate([cot[:, (i ^ 1) * n:((i ^ 1) + 1) * n] for i in range(8)], axis=1)
        rows = rows_ref[...].reshape(tokens, rows_ref.shape[-1])
        g[...] = jnp.dot(cot, rows, preferred_element_type=jnp.float32)
    new_columns(scale, weight_ref, out_ref, products)


def update_together(cots, gathered, weight_t, out, first_column, tile, scale):
    rows, columns = weight_t.shape
    n, _, t, width = gathered.shape
    base = first_column // tile
    whole = pl.BlockSpec((rows, n * t), lambda j: (0, 0))
    here = pl.BlockSpec((rows, tile), lambda j: (0, base + j))
    parts = [pl.BlockSpec((n, 1, t, tile), lambda j, r=r: (0, r, 0, j)) for r in range(3)]
    return pl.pallas_call(
        lambda *refs: together_kernel(scale, *refs),
        grid=(width // tile,),
        in_specs=[whole] * 3 + parts + [here, pl.BlockSpec(memory_space=pl.ANY)],
        out_specs=here,
        out_shape=jax.ShapeDtypeStruct((rows, columns), jnp.float32),
        scratch_shapes=[pltpu.VMEM((rows, tile), jnp.float32)] * 3,
        input_output_aliases={7: 0},
        compiler_params=pltpu.CompilerParams(dimension_semantics=("arbitrary",), vmem_limit_bytes=60 * 2**20),
        cost_estimate=pl.CostEstimate(
            flops=3 * 2 * rows * n * t * width, bytes_accessed=3 * n * t * width * 2 + rows * width * 6, transcendentals=0
        ),
    )(*cots, gathered, gathered, gathered, weight_t, out)


def update(core, cots, first, offset, own2, own3, other2, other3, weight_t, out, first_column, tile, scale):
    rows, columns = weight_t.shape
    tokens, width = own2.shape[0], 2 * own2.shape[1]
    tiles = width // 2 // tile
    base = first_column // tile

    def half_at(i, j, core):
        return (core[0] ^ i) * tiles + j

    whole = pl.BlockSpec((rows, tokens), lambda i, j, core: (0, 0))
    mine = pl.BlockSpec((tokens, tile), lambda i, j, core: (0, jnp.where(i == 0, j, tiles - 1)))
    theirs = pl.BlockSpec((tokens, tile), lambda i, j, core: (0, jnp.where(i == 0, 0, j)))
    here = pl.BlockSpec((rows, tile), lambda i, j, core: (0, base + half_at(i, j, core)))
    args = [core, *cots, first, own2, own3, other2, other3, weight_t]
    specs = [whole] * 3 + [pl.BlockSpec((tokens, tile), lambda i, j, core: (0, offset // tile + half_at(i, j, core)))]
    specs += [mine] * 2 + [theirs] * 2 + [here]
    aliases = {}
    if out is not None:
        aliases = {len(args): 0}
        args.append(out)
        specs.append(pl.BlockSpec(memory_space=pl.ANY))
    return pl.pallas_call(
        lambda *refs: update_kernel(scale, *refs),
        grid_spec=pltpu.PrefetchScalarGridSpec(
            num_scalar_prefetch=1, grid=(2, tiles), in_specs=specs, out_specs=here,
            scratch_shapes=[pltpu.VMEM((rows, tile), jnp.float32)] * 3,
        ),
        out_shape=jax.ShapeDtypeStruct((rows, columns), jnp.float32),
        input_output_aliases=aliases,
        compiler_params=pltpu.CompilerParams(
            dimension_semantics=("arbitrary", "arbitrary"), vmem_limit_bytes=60 * 2**20
        ),
        cost_estimate=pl.CostEstimate(
            flops=3 * 2 * rows * tokens * width,
            bytes_accessed=3 * tokens * width * 2 + rows * width * 6,
            transcendentals=0,
        ),
    )(*args)


def body(context, cotangent, weight):
    tokens, width = context.shape
    scale = width ** (-0.5)
    c = lax.axis_index("c")
    weight_t = weight.T
    block = weight_t.shape[0]
    half = width // 2
    core = c.astype(jnp.int32)[None]

    n = len(CHUNKS)
    starts = [sum(CHUNKS[:i]) for i in range(n)]
    sum_starts = [sum(s[0] for s in SUMS[:i]) for i in range(len(SUMS))]
    group_of = {k: g for g, (ks, _, _) in enumerate(GATHERS) for k in ks}
    offset = {k: starts[k] - starts[GATHERS[group_of[k]][0][0]] for k in range(n)}

    def piece(g, context):
        first, last = GATHERS[g][0][0], GATHERS[g][0][-1]
        return context[:, starts[first]:starts[last] + CHUNKS[last]]

    def half_of(k, gathered):
        first, middle, end = offset[k], offset[k] + CHUNKS[k] // 2, offset[k] + CHUNKS[k]
        return jnp.where(c == 0, gathered[:, first:middle], gathered[:, middle:end])

    live, flying = {"context": context, "cotangent": cotangent, "weight": weight_t}, {}
    for slot in range(n + 3):
        new = {}
        def get(*name):
            name = name if len(name) > 1 else name[0]
            return new[name] if name in new else live[name]

        for g, (_, begin, end) in enumerate(GATHERS):
            if slot == max(begin - 1, 0):
                new["piece", g] = piece(g, live["context"])
            if slot == begin:
                ready = live["piece", g] if ("piece", g) in live else new["piece", g]
                flying["first", g] = lax.all_gather(ready, LOCAL, axis=0, tiled=True)
            if slot == end:
                new["first", g] = flying.pop(("first", g))
        k = slot - 1
        if 0 <= k < n:
            new["own2", k] = hop(live["half", k], "m")
        k = slot - 2
        if 0 <= k < n:
            new["own3", k] = hop(live["own2", k], "x")
            new["other2", k] = hop(live["own2", k], "c")
        k = slot - 3
        if 0 <= k < n:
            new["other3", k] = hop(live["own3", k], "c")
        k = slot
        if k < n:
            at = group_of[k]
            new["half", k] = half_of(k, live["first", at] if ("first", at) in live else new["first", at])
        for k in range(n):
            if slot == (k + 4 if k < n - 3 else k + 3):
                first, own2, own3, other2 = (live[name, k] for name in ("own2", "own2", "own3", "other2"))
                first = live["first", group_of[k]]
                other3 = live["other3", k] if ("other3", k) in live else new["other3", k]
                new["out"] = update(
                    core, live["cots"], first, offset[k], own2, own3, other2, other3, live["weight"],
                    new.get("out", live.get("out")), starts[k], 512, scale
                )

        if slot == 0:
            new["rows2"] = hop(context[:, sum(CHUNKS):], "m")
        if slot == 1:
            new["rows3"] = hop(live["rows2"], "x")
        if slot == 2:
            new["rows"] = jnp.stack([live["context"][:, sum(CHUNKS):], live["rows2"], live["rows3"]])
        if slot == TOGETHER[0]:
            flying["together"] = lax.all_gather(live["rows"], LOCAL, axis=0, tiled=False)
        if slot == TOGETHER[1]:
            new["together"] = flying.pop("together")
        if slot == TOGETHER[1] + 1:
            new["out"] = update_together(
                live["cots"], live["together"], live["weight"], get("out"), sum(CHUNKS), 512, scale
            )

        if slot == 0:
            def columns_of(shard):
                by_block = shard.reshape(tokens, 16, block).transpose(1, 0, 2)
                blocks = lax.all_to_all(by_block, LOCAL, split_axis=0, concat_axis=0, tiled=True)
                return blocks

            cot2 = hop(cotangent, "m")
            blocks = columns_of(cot2).reshape(4, 2, 2 * tokens, block)
            new["cot2_t"] = jnp.stack([blocks[:, 1], blocks[:, 0]], axis=1).reshape(16 * tokens, block).T
            new["weight_sent"] = jnp.where(c == 0, weight_t[:, half:], weight_t[:, :half])
            sizes = jnp.stack([jnp.max(jnp.abs(cotangent)), jnp.max(jnp.abs(weight_t))]).astype(jnp.float32)
            sizes = jnp.broadcast_to(jnp.maximum(sizes, 2.0**-120)[:, None], (2, 128))
            for which in "czpq":
                sizes = jnp.maximum(sizes, hop(sizes, which))
            new["sizes"] = sizes
        if slot == 1:
            new["cot3_t"] = hop(live["cot2_t"], "x")
        if slot == 2:
            new["cot"] = columns_of(live["cotangent"]).reshape(16 * tokens, block)
            weight_own = jnp.where(c == 0, live["weight"][:, :half], live["weight"][:, half:])
            new["both_weights"] = jnp.concatenate([weight_own, hop(live["weight_sent"], "c")], axis=0)
        if slot == 3:
            new["cots"] = (live["cot"].T, live["cot2_t"], live["cot3_t"])
            new["both_cots"] = jnp.concatenate([live["cot"], hop(live["cot"], "c")], axis=1)
        if slot > 1:
            cot_size, weight_size = live["sizes"][0, 0], live["sizes"][1, 0]
        for i, (columns, made, begin, end) in enumerate(SUMS):
            if slot == made:
                part = jnp.dot(
                    get("both_cots"), live["both_weights"][:, sum_starts[i]:sum_starts[i] + columns],
                    preferred_element_type=jnp.float32
                )
                part = (part * (1.0 / cot_size)) * (1.0 / weight_size)
                new["part", i] = part.astype(jnp.float16).reshape(8, 2 * tokens, columns)
            if slot == begin:
                flying["sent", i] = lax.all_to_all(get("part", i), ("y", "zl"), split_axis=0, concat_axis=0, tiled=True)
            if slot == end:
                new["sent", i] = flying.pop(("sent", i))
            if slot == end + 1:
                total = jnp.sum(live["sent", i].astype(jnp.float32), axis=0) * (cot_size * scale) * weight_size
                new["sum", i] = total.astype(jnp.bfloat16)
        if slot == n + 2:
            summed = jnp.concatenate([get("sum", i) for i in range(len(SUMS))], axis=1)
            mine = lax.dynamic_slice_in_dim(summed, c * tokens, tokens, axis=0)
            arrived = hop(lax.dynamic_slice_in_dim(summed, (1 - c) * tokens, tokens, axis=0), "c")
            new["input_grad"] = jnp.where(
                c == 0,
                jnp.concatenate([mine, arrived], axis=1),
                jnp.concatenate([arrived, mine], axis=1),
            )
        live.update(new)
        if slot < n + 2:
            names = list(live)
            live = dict(zip(names, lax.optimization_barrier(tuple(live[name] for name in names))))
    return live["input_grad"], live["out"].T[None]


def solution(mesh):
    sub = Mesh(mesh.devices.reshape(SIZES), AXES)
    tokens = P(AXES, None)
    return jax.shard_map(
        body,
        mesh=sub,
        in_specs=(tokens, tokens, P(None, LOCAL)),
        out_specs=(tokens, P(("x", "zh"), None, LOCAL)),
        check_vma=False,
    )
```

```python
import jax
import jax.numpy as jnp
from jax import lax
from jax.experimental import pallas as pl
from jax.experimental.pallas import tpu as pltpu
from jax.sharding import Mesh, PartitionSpec as P

AXES = ("x", "zh", "y", "zl", "c")
SIZES = (4, 2, 4, 2, 2)
LOCAL = ("y", "zl", "c")

CHUNKS = (1024,) * 6
GATHERS = (((0, 1), 0, 0), ((2, 3, 4), 1, 2), ((5,), 3, 5))
TOGETHER = (4, 6)
SUMS = ((1536, 3, 3, 5), (2048, 4, 6, 7))


def hop(block, which):
    if which == "p":
        return lax.ppermute(block, "y", [(i, i ^ 1) for i in range(4)])
    if which == "q":
        return lax.ppermute(block, "y", [(i, 3 - i) for i in range(4)])
    if which == "z":
        return lax.ppermute(block, "zl", [(0, 1), (1, 0)])
    if which == "m":
        return lax.ppermute(block, ("zh", "zl"), [(i, 3 - i) for i in range(4)])
    if which == "h":
        return lax.ppermute(block, "zh", [(0, 1), (1, 0)])
    if which == "x":
        route = [(2 * i, 2 * ((i + 1) % 4)) for i in range(4)]
        route += [(2 * i + 1, 2 * ((i + 3) % 4) + 1) for i in range(4)]
        return lax.ppermute(block, ("x", "zh"), route)
    return lax.ppermute(block, "c", [(0, 1), (1, 0)])


def new_columns(scale, weight_ref, out_ref, products):
    rows = out_ref.shape[0]
    step_rows = 32
    stats = []
    for g in products:
        top = bottom = g[0:8, :]
        for r in range(8, rows, 8):
            piece = g[r:r + 8, :]
            top, bottom = jnp.maximum(top, piece), jnp.minimum(bottom, piece)
        top = jnp.max(top, axis=0, keepdims=True)
        spread = top - jnp.min(bottom, axis=0, keepdims=True)
        stats.append((top, 1.0 / spread, spread * (0.25 * scale / (3.0 * 255.0))))
    low = sum(top for top, _, _ in stats) * (-0.25 * scale / 3.0)
    for r in range(0, rows, step_rows):
        here = slice(r, r + step_rows)
        total = weight_ref[here, :].astype(jnp.float32) + low
        for g, (top, inverse, step) in zip(products, stats):
            code = (((top - g[here, :]) * inverse) * 255.0).astype(jnp.bfloat16)
            total += code.astype(jnp.float32) * step
        out_ref[here, :] = total


def update_kernel(scale, core, cot1, cot2, cot3, first, own2, own3, other2, other3, weight_ref, *rest):
    out_ref, *products = rest[-4:]

    def run(second, third):
        for g, cot_ref, rows_ref in zip(products, (cot1, cot2, cot3), (first, second, third)):
            g[...] = jnp.dot(cot_ref[...], rows_ref[...], preferred_element_type=jnp.float32)
        new_columns(scale, weight_ref, out_ref, products)

    @pl.when(pl.program_id(0) == 0)
    def _():
        run(own2, own3)

    @pl.when(pl.program_id(0) == 1)
    def _():
        run(other2, other3)


def together_kernel(scale, cot1, cot2, cot3, first, second, third, weight_ref, *rest):
    out_ref, *products = rest[-4:]
    tokens = cot1.shape[1]
    n = tokens // 8
    for g, cot_ref, rows_ref, swap in zip(products, (cot1, cot2, cot3), (first, second, third), (0, 1, 1)):
        cot = cot_ref[...]
        if swap:
            cot = jnp.concatenate([cot[:, (i ^ 1) * n:((i ^ 1) + 1) * n] for i in range(8)], axis=1)
        rows = rows_ref[...].reshape(tokens, rows_ref.shape[-1])
        g[...] = jnp.dot(cot, rows, preferred_element_type=jnp.float32)
    new_columns(scale, weight_ref, out_ref, products)


def update_together(cots, gathered, weight_t, out, first_column, tile, scale):
    rows, columns = weight_t.shape
    n, _, t, width = gathered.shape
    base = first_column // tile
    whole = pl.BlockSpec((rows, n * t), lambda j: (0, 0))
    here = pl.BlockSpec((rows, tile), lambda j: (0, base + j))
    parts = [pl.BlockSpec((n, 1, t, tile), lambda j, r=r: (0, r, 0, j)) for r in range(3)]
    return pl.pallas_call(
        lambda *refs: together_kernel(scale, *refs),
        grid=(width // tile,),
        in_specs=[whole] * 3 + parts + [here, pl.BlockSpec(memory_space=pl.ANY)],
        out_specs=here,
        out_shape=jax.ShapeDtypeStruct((rows, columns), jnp.float32),
        scratch_shapes=[pltpu.VMEM((rows, tile), jnp.float32)] * 3,
        input_output_aliases={7: 0},
        compiler_params=pltpu.CompilerParams(dimension_semantics=("arbitrary",), vmem_limit_bytes=60 * 2**20),
        cost_estimate=pl.CostEstimate(
            flops=3 * 2 * rows * n * t * width, bytes_accessed=3 * n * t * width * 2 + rows * width * 6, transcendentals=0
        ),
    )(*cots, gathered, gathered, gathered, weight_t, out)


def update(core, cots, first, offset, own2, own3, other2, other3, weight_t, out, first_column, tile, scale):
    rows, columns = weight_t.shape
    tokens, width = own2.shape[0], 2 * own2.shape[1]
    tiles = width // 2 // tile
    base = first_column // tile

    def half_at(i, j, core):
        return (core[0] ^ i) * tiles + j

    whole = pl.BlockSpec((rows, tokens), lambda i, j, core: (0, 0))
    mine = pl.BlockSpec((tokens, tile), lambda i, j, core: (0, jnp.where(i == 0, j, tiles - 1)))
    theirs = pl.BlockSpec((tokens, tile), lambda i, j, core: (0, jnp.where(i == 0, 0, j)))
    here = pl.BlockSpec((rows, tile), lambda i, j, core: (0, base + half_at(i, j, core)))
    args = [core, *cots, first, own2, own3, other2, other3, weight_t]
    specs = [whole] * 3 + [pl.BlockSpec((tokens, tile), lambda i, j, core: (0, offset // tile + half_at(i, j, core)))]
    specs += [mine] * 2 + [theirs] * 2 + [here]
    aliases = {}
    if out is not None:
        aliases = {len(args): 0}
        args.append(out)
        specs.append(pl.BlockSpec(memory_space=pl.ANY))
    return pl.pallas_call(
        lambda *refs: update_kernel(scale, *refs),
        grid_spec=pltpu.PrefetchScalarGridSpec(
            num_scalar_prefetch=1, grid=(2, tiles), in_specs=specs, out_specs=here,
            scratch_shapes=[pltpu.VMEM((rows, tile), jnp.float32)] * 3,
        ),
        out_shape=jax.ShapeDtypeStruct((rows, columns), jnp.float32),
        input_output_aliases=aliases,
        compiler_params=pltpu.CompilerParams(
            dimension_semantics=("arbitrary", "arbitrary"), vmem_limit_bytes=60 * 2**20
        ),
        cost_estimate=pl.CostEstimate(
            flops=3 * 2 * rows * tokens * width,
            bytes_accessed=3 * tokens * width * 2 + rows * width * 6,
            transcendentals=0,
        ),
    )(*args)


def body(context, cotangent, weight):
    tokens, width = context.shape
    scale = width ** (-0.5)
    c = lax.axis_index("c")
    weight_t = weight.T
    block = weight_t.shape[0]
    half = width // 2
    core = c.astype(jnp.int32)[None]

    n = len(CHUNKS)
    starts = [sum(CHUNKS[:i]) for i in range(n)]
    sum_starts = [sum(s[0] for s in SUMS[:i]) for i in range(len(SUMS))]
    group_of = {k: g for g, (ks, _, _) in enumerate(GATHERS) for k in ks}
    offset = {k: starts[k] - starts[GATHERS[group_of[k]][0][0]] for k in range(n)}

    def piece(g, context):
        first, last = GATHERS[g][0][0], GATHERS[g][0][-1]
        return context[:, starts[first]:starts[last] + CHUNKS[last]]

    def half_of(k, gathered):
        first, middle, end = offset[k], offset[k] + CHUNKS[k] // 2, offset[k] + CHUNKS[k]
        return jnp.where(c == 0, gathered[:, first:middle], gathered[:, middle:end])

    live, flying = {"context": context, "cotangent": cotangent, "weight": weight_t}, {}
    for slot in range(n + 3):
        new = {}
        def get(*name):
            name = name if len(name) > 1 else name[0]
            return new[name] if name in new else live[name]

        for g, (_, begin, end) in enumerate(GATHERS):
            if slot == max(begin - 1, 0):
                new["piece", g] = piece(g, live["context"])
            if slot == begin:
                ready = live["piece", g] if ("piece", g) in live else new["piece", g]
                flying["first", g] = lax.all_gather(ready, LOCAL, axis=0, tiled=True)
            if slot == end:
                new["first", g] = flying.pop(("first", g))
        k = slot - 1
        if 0 <= k < n:
            new["own2", k] = hop(live["half", k], "m")
        k = slot - 2
        if 0 <= k < n:
            new["own3", k] = hop(live["own2", k], "x")
            new["other2", k] = hop(live["own2", k], "c")
        k = slot - 3
        if 0 <= k < n:
            new["other3", k] = hop(live["own3", k], "c")
        k = slot
        if k < n:
            at = group_of[k]
            new["half", k] = half_of(k, live["first", at] if ("first", at) in live else new["first", at])
        for k in range(n):
            if slot == (k + 4 if k < n - 3 else k + 3):
                first, own2, own3, other2 = (live[name, k] for name in ("own2", "own2", "own3", "other2"))
                first = live["first", group_of[k]]
                other3 = live["other3", k] if ("other3", k) in live else new["other3", k]
                new["out"] = update(
                    core, live["cots"], first, offset[k], own2, own3, other2, other3, live["weight"],
                    new.get("out", live.get("out")), starts[k], 512, scale
                )

        if slot == 0:
            new["rows2"] = hop(context[:, sum(CHUNKS):], "m")
        if slot == 1:
            new["rows3"] = hop(live["rows2"], "x")
        if slot == 2:
            new["rows"] = jnp.stack([live["context"][:, sum(CHUNKS):], live["rows2"], live["rows3"]])
        if slot == TOGETHER[0]:
            flying["together"] = lax.all_gather(live["rows"], LOCAL, axis=0, tiled=False)
        if slot == TOGETHER[1]:
            new["together"] = flying.pop("together")
        if slot == TOGETHER[1] + 1:
            new["out"] = update_together(
                live["cots"], live["together"], live["weight"], get("out"), sum(CHUNKS), 512, scale
            )

        if slot == 0:
            def columns_of(shard):
                by_block = shard.reshape(tokens, 16, block).transpose(1, 0, 2)
                blocks = lax.all_to_all(by_block, LOCAL, split_axis=0, concat_axis=0, tiled=True)
                return blocks

            cot2 = hop(cotangent, "m")
            blocks = columns_of(cot2).reshape(4, 2, 2 * tokens, block)
            new["cot2_t"] = jnp.stack([blocks[:, 1], blocks[:, 0]], axis=1).reshape(16 * tokens, block).T
            weight_own = jnp.where(c == 0, weight_t[:, :half], weight_t[:, half:])
            weight_sent = jnp.where(c == 0, weight_t[:, half:], weight_t[:, :half])
            new["both_weights"] = jnp.concatenate([weight_own, hop(weight_sent, "c")], axis=0)
            sizes = jnp.stack([jnp.max(jnp.abs(cotangent)), jnp.max(jnp.abs(weight_t))]).astype(jnp.float32)
            sizes = jnp.broadcast_to(jnp.maximum(sizes, 2.0**-120)[:, None], (2, 128))
            for which in "czpq":
                sizes = jnp.maximum(sizes, hop(sizes, which))
            new["sizes"] = sizes
        if slot == 1:
            new["cot3_t"] = hop(live["cot2_t"], "x")
        if slot == 2:
            new["cot"] = columns_of(live["cotangent"]).reshape(16 * tokens, block)
        if slot == 3:
            new["cots"] = (live["cot"].T, live["cot2_t"], live["cot3_t"])
            new["both_cots"] = jnp.concatenate([live["cot"], hop(live["cot"], "c")], axis=1)
        if slot > 1:
            cot_size, weight_size = live["sizes"][0, 0], live["sizes"][1, 0]
        for i, (columns, made, begin, end) in enumerate(SUMS):
            if slot == made:
                part = jnp.dot(
                    get("both_cots"), live["both_weights"][:, sum_starts[i]:sum_starts[i] + columns],
                    preferred_element_type=jnp.float32
                )
                part = (part * (1.0 / cot_size)) * (1.0 / weight_size)
                new["part", i] = part.astype(jnp.float16).reshape(8, 2 * tokens, columns)
            if slot == begin:
                flying["sent", i] = lax.all_to_all(get("part", i), ("y", "zl"), split_axis=0, concat_axis=0, tiled=True)
            if slot == end:
                new["sent", i] = flying.pop(("sent", i))
            if slot == end + 1:
                total = jnp.sum(live["sent", i].astype(jnp.float32), axis=0) * (cot_size * scale) * weight_size
                new["sum", i] = total.astype(jnp.bfloat16)
        if slot == n + 2:
            summed = jnp.concatenate([get("sum", i) for i in range(len(SUMS))], axis=1)
            mine = lax.dynamic_slice_in_dim(summed, c * tokens, tokens, axis=0)
            arrived = hop(lax.dynamic_slice_in_dim(summed, (1 - c) * tokens, tokens, axis=0), "c")
            new["input_grad"] = jnp.where(
                c == 0,
                jnp.concatenate([mine, arrived], axis=1),
                jnp.concatenate([arrived, mine], axis=1),
            )
        live.update(new)
        if slot < n + 2:
            names = list(live)
            live = dict(zip(names, lax.optimization_barrier(tuple(live[name] for name in names))))
    return live["input_grad"], live["out"].T[None]


def solution(mesh):
    sub = Mesh(mesh.devices.reshape(SIZES), AXES)
    tokens = P(AXES, None)
    return jax.shard_map(
        body,
        mesh=sub,
        in_specs=(tokens, tokens, P(None, LOCAL)),
        out_specs=(tokens, P(("x", "zh"), None, LOCAL)),
        check_vma=False,
    )
```
